256 devices in a mesh: src: 8 (over x, y_hi), dst: 32 (over z, y_lo, core).
Axes of the slice: x: 4, y: 4 (y_hi: 2, y_lo: 2; y = y_hi * 2 + y_lo), z: 8, core: 2. Of those that a mesh axis runs over, the one named last changes fastest.
Arguments:
- edge_in: bfloat16 [1048576, 512], P(('src', 'dst')), may hold values from -6 to 6
- atom_in: bfloat16 [16384, 256], P(('dst', 'src')), may hold values from -6 to 6
- targets: int32 [1048576], P(('src', 'dst')), may hold values from 0 to 511
- reverse: int32 [1048576], P(('src', 'dst')), may hold values from 0 to 127, as said below
- counts: int32 [8, 32, 32], P('src', 'dst'), may hold values from 2 to 128, as said below
- w_in: bfloat16 [256, 512], replicated, may hold values from -0.375 to 0.375
- gains: float32 [2, 512], replicated, may hold values from 0.1 to 1.9
- w_layers: bfloat16 [2, 512, 512], replicated, may hold values from -0.25 to 0.25
- w_rev: bfloat16 [512, 512], replicated, may hold values from -0.25 to 0.25
- w_down: bfloat16 [512, 256], replicated, may hold values from -0.25 to 0.25
- w_atom: bfloat16 [256, 256], replicated, may hold values from -0.375 to 0.375
Outputs:
- edge_out: bfloat16 [1048576, 512], P(('src', 'dst'))
- atom_out: bfloat16 [16384, 256], P(('dst', 'src'))
The draws below stay inside these ranges and needn't reach their ends.
Inputs may be any that keep to these rules, and one draw needn't show every extreme that they name: In every block k of tile (i, j), reverse maps the used slots one to one onto the used slots of block j of tile (i, k), and the two maps are inverse to each other; in block j of tile (i, j) it pairs used slots and is its own inverse. Unused slots map onto unused slots. Every count is even, and counts[i, j, k] equals counts[i, k, j].
All inputs are finite; a program needn't handle non-finite values.
Results may differ from the reference program's by a relative error of at most 0.014.
Values may be sent and summed in bfloat16 or wider, within the bound.
A program may use at most 128 MiB of HBM per device.

```python
import jax
import jax.numpy as jnp
from jax import lax

W = 512
A = 256
LAYERS = 2
RB = 128
EDGE_DEV = 4096
EDGES = 1048576
ATOM_PART = 512
ATOMS = 16384
N_SRC = 8
N_DST = 32


def mirror_tables(key):
    base = jax.random.fold_in(key, 7)
    key_count, key_order = jax.random.split(base, 2)
    lowest = max(1, RB // 16)
    raw = jax.random.randint(key_count, (N_SRC, N_DST, N_DST), lowest, RB // 2 + 1) * 2
    rows_j = jnp.arange(N_DST)[:, None]
    cols_k = jnp.arange(N_DST)[None, :]
    count = jnp.where(rows_j <= cols_k, raw, jnp.transpose(raw, (0, 2, 1))).astype(jnp.int32)
    slot = jnp.arange(RB).astype(jnp.int32)
    noise = jax.random.randint(key_order, (N_SRC, N_DST, N_DST, RB), 0, 2 ** 14)
    scores = (slot >= count[..., None]).astype(jnp.int32) * 2 ** 24 + noise * RB + slot
    order = jnp.argsort(scores, axis=-1, stable=True).astype(jnp.int32)
    other = jnp.transpose(order, (0, 2, 1, 3))
    partner = order[..., jnp.bitwise_xor(slot, 1)]
    diagonal = (rows_j == cols_k)[None, :, :, None]
    value = jnp.where(diagonal, partner, other)
    inverse = jnp.argsort(order, axis=-1, stable=True).astype(jnp.int32)
    back = jnp.take_along_axis(value, inverse, axis=-1).astype(jnp.int32)
    return (back.reshape(N_SRC * N_DST * N_DST * RB), count)


def draw_reverse(key, part):
    return mirror_tables(key)[0]


def draw_counts(key, part):
    return mirror_tables(key)[1]


def touch_ends(values, own_key, least, high):
    longest = values.shape.index(max(values.shape))
    spots = []
    for shift in (0, 1):
        where = [jax.random.randint(jax.random.fold_in(own_key, axis), (), 0, length) for axis, length in enumerate(values.shape)]
        where[longest] = (where[longest] + shift) % values.shape[longest]
        spots.append(tuple(where))
    return values.at[spots[0]].set(least).at[spots[1]].set(high)


def block_scale(own_key, extent, cuts, smallest, top_value):
    level, own = 1.0, jax.random.fold_in(own_key, 6)
    for axis_at, parts in cuts:
        draws = jnp.exp(jax.random.uniform(jax.random.fold_in(own, axis_at), (parts,), jnp.float32, smallest / len(cuts), top_value / len(cuts)))
        level = level * jnp.repeat(draws, extent[axis_at] // parts).reshape([-1 if axis == axis_at else 1 for axis in range(len(extent))])
    return level


def scatter_about(rng, dims, scale, limit, pieces=(), held_as=jnp.bfloat16):
    factor_of = block_scale(rng, dims, pieces, -0.22, 0.18) if pieces else 1.0
    entries = jax.random.normal(rng, dims, jnp.float32) * scale * factor_of
    return jnp.minimum(jnp.maximum(entries, -limit), limit).astype(held_as)


def setup_inputs(seed: int = 0) -> dict:
    splits = jax.random.split(jax.random.key(seed), 12)
    return {
        "edge_in": scatter_about(splits[0], (EDGES, W), 1.0, 6.0, ((0, 256),)),
        "atom_in": scatter_about(splits[1], (ATOMS, A), 1.0, 6.0, ((0, 256),)),
        "targets": touch_ends(jax.random.randint(splits[2], (EDGES,), 0, ATOM_PART), jax.random.fold_in(splits[2], 1), 0, ATOM_PART - 1).astype(jnp.int32),
        "reverse": draw_reverse(jax.random.fold_in(splits[11], 71), 0),
        "counts": draw_counts(jax.random.fold_in(splits[11], 71), 0),
        "w_in": scatter_about(splits[5], (A, W), A ** -0.5, 0.375),
        "gains": jnp.clip(1.0 + 0.18 * jax.random.normal(splits[6], (LAYERS, W), jnp.float32), 0.1, 1.9),
        "w_layers": scatter_about(splits[7], (LAYERS, W, W), W ** -0.5, 0.25),
        "w_rev": scatter_about(splits[8], (W, W), W ** -0.5, 0.25),
        "w_down": scatter_about(splits[9], (W, A), W ** -0.5, 0.25),
        "w_atom": scatter_about(splits[10], (A, A), A ** -0.5, 0.375),
    }


def edge_layers(base, picked, gains, w_layers):
    state = base.astype(jnp.float32) + picked.astype(jnp.float32)
    for layer in range(LAYERS):
        scale = lax.rsqrt(lax.optimization_barrier(jnp.mean(state * state, axis=-1, keepdims=True)) + 1e-06)
        normed = (state * scale * gains[layer]).astype(jnp.bfloat16)
        state = state + jax.nn.silu(jnp.dot(normed, w_layers[layer], preferred_element_type=jnp.float32))
    return state

def reference(edge_in, atom_in, targets, reverse, counts, w_in, gains, w_layers, w_rev, w_down, w_atom):
    row_len = N_DST * EDGE_DEV
    atom_proj = jnp.dot(atom_in, w_in, preferred_element_type=jnp.float32).astype(jnp.bfloat16)
    place = jnp.arange(row_len).astype(jnp.int32)
    column = place // EDGE_DEV
    block = place % EDGE_DEV // RB
    slot = place % RB

    def one_row(total, item):
        edges, targ, back, count = item
        used = slot < count[column, block]
        atom_ids = (column * ATOM_PART + targ).astype(jnp.int32)
        picked = jnp.take(atom_proj, atom_ids, axis=0)
        state = edge_layers(edges, picked, gains, w_layers)
        sent = state.astype(jnp.bfloat16)
        source = (block * EDGE_DEV + column * RB + back).astype(jnp.int32)
        mirrored = jnp.take(sent, source, axis=0)
        combined = jnp.where(used[:, None], state + jnp.dot(mirrored, w_rev, preferred_element_type=jnp.float32), jnp.float32(0.0))
        result = combined.astype(jnp.bfloat16)
        contrib = jnp.where(used[:, None], jnp.dot(result, w_down, preferred_element_type=jnp.float32), jnp.float32(0.0))
        total = total + jax.ops.segment_sum(contrib, atom_ids, num_segments=ATOMS)
        return (total, result)
    items = (edge_in.reshape(N_SRC, row_len, W), targets.reshape(N_SRC, row_len), reverse.reshape(N_SRC, row_len), counts)
    agg, outs = lax.scan(one_row, jnp.zeros((ATOMS, A), jnp.float32), items)
    act = jax.nn.silu(0.3 * agg).astype(jnp.bfloat16)
    atom_out = (atom_in.astype(jnp.float32) + jnp.dot(act, w_atom, preferred_element_type=jnp.float32)).astype(jnp.bfloat16)
    return (outs.reshape(EDGES, W), atom_out)
```

```python
import functools

import jax
import jax.numpy as jnp
from jax import lax
from jax.experimental import pallas as pl
from jax.experimental.pallas import tpu as pltpu
from jax.sharding import PartitionSpec as P

MESH = pl.DeviceIdType.MESH
RB = 128
PLANE = 4


def silu(v):
    half = 0.5 * v
    return half + half * jnp.tanh(half)


def kernel(
    n_src, n_dst,
    edge_ref, atom_ref, targ_ref, rev_ref, cnt_ref, w_in_ref, gains_ref, w_lay_ref, w_rev_ref, w_down_ref, w_atom_ref,
    edge_out_ref, atom_out_ref,
    edges, xs, send, recv, atoms, proj, w_in, w_lay, w_rev, w_down, w_atom, seg, part, parts,
    in_sem, w_sem, at_send, at_recv, send_sem, recv_sem, out_sem, pt_send, pt_recv,
):
    planes = n_dst // PLANE
    width = edges.shape[1]
    layers = w_lay.shape[0]
    n_atoms = proj.shape[0]
    chunk = PLANE * RB
    row = lax.axis_index("src")
    me = lax.axis_index("dst")
    z = me // PLANE

    barrier = pltpu.get_barrier_semaphore()

    @pl.loop(1, n_src)
    def _(d):
        pl.semaphore_signal(barrier, inc=1, device_id={"src": lax.rem(row + d, n_src)}, device_id_type=MESH)

    @pl.loop(1, n_dst)
    def _(d):
        pl.semaphore_signal(barrier, inc=1, device_id={"dst": lax.rem(me + d, n_dst)}, device_id_type=MESH)

    def out_plane(n):
        dz = jnp.where(n % 2 == 0, planes // 2 + n // 2, planes // 2 - 1 - n // 2)
        return lax.rem(z + dz, planes)

    def in_plane(n):
        dz = jnp.where(n % 2 == 0, planes // 2 - n // 2, planes // 2 + 1 + n // 2)
        return lax.rem(z + dz, planes)

    def rows_of(zp):
        return pl.ds(pl.multiple_of(zp * chunk, chunk), chunk)

    def edge_load(zp):
        return pltpu.make_async_copy(edge_ref.at[rows_of(zp)], edges.at[rows_of(zp)], in_sem.at[zp])

    weight_loads = [
        pltpu.make_async_copy(src, dst, w_sem.at[i])
        for i, (src, dst) in enumerate(
            [(w_in_ref, w_in), (w_lay_ref, w_lay), (w_rev_ref, w_rev), (w_down_ref, w_down), (w_atom_ref, w_atom)]
        )
    ]
    own_atoms = pltpu.make_async_copy(atom_ref, atoms.at[row], w_sem.at[5])
    own_atoms.start()
    weight_loads[0].start()
    weight_loads[1].start()

    @pl.loop(0, planes)
    def _(n):
        edge_load(out_plane(n)).start()

    for load in weight_loads[2:]:
        load.start()
    seg[...] = jnp.zeros_like(seg)

    pl.semaphore_wait(barrier, n_src + n_dst - 2)

    def atom_copy(d):
        return pltpu.make_async_remote_copy(
            src_ref=atom_ref, dst_ref=atoms.at[row], send_sem=at_send.at[d], recv_sem=at_recv.at[d],
            device_id={"src": lax.rem(row + d, n_src)}, device_id_type=MESH,
        )

    @pl.loop(1, n_src)
    def _(d):
        atom_copy(d).start()

    weight_loads[0].wait()
    weight_loads[1].wait()
    own_atoms.wait()

    @pl.loop(1, n_src)
    def _(d):
        atom_copy(d).wait()

    whole = atoms[...].reshape(n_atoms, atoms.shape[2])
    proj[...] = jnp.dot(whole, w_in[...], preferred_element_type=jnp.float32).astype(jnp.bfloat16)

    def block_copy(k):
        return pltpu.make_async_remote_copy(
            src_ref=send.at[k], dst_ref=recv.at[me], send_sem=send_sem.at[k], recv_sem=recv_sem.at[me],
            device_id={"dst": k}, device_id_type=MESH,
        )

    def arrival(k):
        return pltpu.make_async_remote_copy(
            src_ref=send.at[k], dst_ref=recv.at[k], send_sem=send_sem.at[k], recv_sem=recv_sem.at[k],
            device_id={"dst": k}, device_id_type=MESH,
        )

    def own_copy():
        return pltpu.make_async_copy(send.at[me], recv.at[me], recv_sem.at[me])

    @pl.loop(0, planes)
    def _(n):
        zp = out_plane(n)
        edge_load(zp).wait()
        hot = []
        targ = targ_ref[zp]
        for q in range(PLANE):
            col = jnp.broadcast_to(targ[q : q + 1, :], (RB, RB)).T
            lane = lax.broadcasted_iota(jnp.int32, (RB, RB), 1)
            hot.append(
                jnp.concatenate(
                    [(col == lane + p * RB).astype(jnp.float32).astype(jnp.bfloat16) for p in range(n_atoms // RB)], axis=1
                )
            )
        picked = jnp.dot(jnp.concatenate(hot, axis=0), proj[...], preferred_element_type=jnp.float32)
        x = edges[rows_of(zp), :].astype(jnp.float32) + picked
        for layer in range(layers):
            scale = lax.rsqrt(jnp.mean(x * x, axis=-1, keepdims=True) + 1e-6)
            normed = (x * scale * gains_ref[layer : layer + 1, :]).astype(jnp.bfloat16)
            x = x + silu(jnp.dot(normed, w_lay[layer], preferred_element_type=jnp.float32))
        xs[rows_of(zp), :] = x
        sent = x.astype(jnp.bfloat16)
        rev = rev_ref[zp]
        for q in range(PLANE):
            k = zp * PLANE + q
            sub = lax.broadcasted_iota(jnp.int32, (RB, RB), 0)
            perm = (sub == rev[q : q + 1, :]).astype(jnp.float32).astype(jnp.bfloat16)
            moved = jnp.dot(perm, sent[q * RB : (q + 1) * RB, :], preferred_element_type=jnp.float32)
            send[k] = moved.astype(jnp.bfloat16)

            @pl.when(k != me)
            def _():
                block_copy(k).start()

            @pl.when(k == me)
            def _():
                own_copy().start()

    for load in weight_loads[2:]:
        load.wait()

    def edge_store(zp):
        return pltpu.make_async_copy(edges.at[rows_of(zp)], edge_out_ref.at[rows_of(zp)], out_sem.at[zp])

    @pl.loop(0, planes)
    def _(n):
        zp = in_plane(n)
        for q in range(PLANE):
            k = zp * PLANE + q

            @pl.when(k != me)
            def _():
                arrival(k).wait_recv()

            @pl.when(k == me)
            def _():
                own_copy().wait()

        came = recv[pl.ds(zp * PLANE, PLANE)].reshape(chunk, width)
        total = xs[rows_of(zp), :] + jnp.dot(came, w_rev[...], preferred_element_type=jnp.float32)
        kept = []
        for q in range(PLANE):
            slot = lax.broadcasted_iota(jnp.int32, (RB, width), 0)
            kept.append(jnp.where(slot < cnt_ref[zp * PLANE + q], total[q * RB : (q + 1) * RB, :], 0.0))
        result = jnp.concatenate(kept, axis=0).astype(jnp.bfloat16)
        edges[rows_of(zp), :] = result
        edge_store(zp).start()
        targ = targ_ref[zp]
        sub = lax.broadcasted_iota(jnp.int32, (n_atoms, RB), 0)
        hot = jnp.concatenate(
            [(sub == targ[q : q + 1, :]).astype(jnp.float32).astype(jnp.bfloat16) for q in range(PLANE)], axis=1
        )
        seg[...] += jnp.dot(hot, result, preferred_element_type=jnp.float32)

    down = jnp.dot(seg[...].astype(jnp.bfloat16), w_down[...], preferred_element_type=jnp.float32)
    part[...] = down.astype(jnp.bfloat16).reshape(part.shape)

    def part_copy(d):
        to = lax.rem(row + d, n_src)
        return pltpu.make_async_remote_copy(
            src_ref=part.at[to], dst_ref=parts.at[d], send_sem=pt_send.at[d], recv_sem=pt_recv.at[d],
            device_id={"src": to}, device_id_type=MESH,
        )

    @pl.loop(1, n_src)
    def _(d):
        part_copy(d).start()

    agg = part[row].astype(jnp.float32)

    @pl.loop(1, n_src)
    def _(d):
        part_copy(d).wait()

    for d in range(1, n_src):
        agg = agg + parts[d].astype(jnp.float32)
    act = silu(0.3 * agg).astype(jnp.bfloat16)
    update = jnp.dot(act, w_atom[...], preferred_element_type=jnp.float32)
    atom_out_ref[...] = (atoms[row].astype(jnp.float32) + update).astype(jnp.bfloat16)

    @pl.loop(0, n_dst)
    def _(k):
        @pl.when(k != me)
        def _():
            arrival(k).wait_send()

    @pl.loop(0, planes)
    def _(n):
        edge_store(n).wait()


def solution(mesh):
    n_src, n_dst = mesh.shape["src"], mesh.shape["dst"]
    planes = n_dst // PLANE

    def on_device(edge_in, atom_in, targets, reverse, counts, w_in, gains, w_layers, w_rev, w_down, w_atom):
        slots, width = edge_in.shape
        own, depth = atom_in.shape
        n_atoms = own * n_src
        bf16, f32 = jnp.bfloat16, jnp.float32
        anywhere = pl.BlockSpec(memory_space=pl.ANY)
        vmem = pl.BlockSpec(memory_space=pltpu.VMEM)
        smem = pl.BlockSpec(memory_space=pltpu.SMEM)
        dma = pltpu.SemaphoreType.DMA
        return pl.pallas_call(
            functools.partial(kernel, n_src, n_dst),
            out_shape=(
                jax.ShapeDtypeStruct(edge_in.shape, bf16),
                jax.ShapeDtypeStruct(atom_in.shape, bf16),
            ),
            in_specs=[anywhere, anywhere, vmem, vmem, smem, anywhere, vmem] + [anywhere] * 4,
            out_specs=(anywhere, vmem),
            scratch_shapes=[
                pltpu.VMEM((slots, width), bf16),
                pltpu.VMEM((slots, width), f32),
                pltpu.VMEM((n_dst, RB, width), bf16),
                pltpu.VMEM((n_dst, RB, width), bf16),
                pltpu.VMEM((n_src, own, depth), bf16),
                pltpu.VMEM((n_atoms, width), bf16),
                pltpu.VMEM(w_in.shape, bf16),
                pltpu.VMEM(w_layers.shape, bf16),
                pltpu.VMEM(w_rev.shape, bf16),
                pltpu.VMEM(w_down.shape, bf16),
                pltpu.VMEM(w_atom.shape, bf16),
                pltpu.VMEM((n_atoms, width), f32),
                pltpu.VMEM((n_src, own, depth), bf16),
                pltpu.VMEM((n_src, own, depth), bf16),
                dma((planes,)),
                dma((6,)),
                dma((n_src,)),
                dma((n_src,)),
                dma((n_dst,)),
                dma((n_dst,)),
                dma((planes,)),
                dma((n_src,)),
                dma((n_src,)),
            ],
            compiler_params=pltpu.CompilerParams(
                collective_id=0, has_side_effects=True, vmem_limit_bytes=56 * 2**20
            ),
        )(
            edge_in, atom_in, targets.reshape(planes, PLANE, RB), reverse.reshape(planes, PLANE, RB), counts.reshape(n_dst),
            w_in, gains, w_layers, w_rev, w_down, w_atom,
        )

    both = ("src", "dst")
    in_specs = (
        P(both, None), P(("dst", "src"), None), P(both), P(both), P("src", "dst", None),
        P(), P(), P(), P(), P(), P(),
    )
    out_specs = (P(both, None), P(("dst", "src"), None))
    return jax.shard_map(on_device, mesh=mesh, in_specs=in_specs, out_specs=out_specs, check_vma=False)
```

```python
import functools

import jax
import jax.numpy as jnp
from jax import lax
from jax.experimental import pallas as pl
from jax.experimental.pallas import tpu as pltpu
from jax.sharding import PartitionSpec as P

MESH = pl.DeviceIdType.MESH
RB = 128
PLANE = 4
AHEAD = 2
BEHIND = 2
VMEM_MIB = 54


def silu(v):
    half = 0.5 * v
    return half + half * jnp.tanh(half)


def far_peer(row, d, way, n_src):
    chips = n_src // 2
    same = d // (chips + 1)
    at = d - 1 - same * chips
    dx = jnp.where(at == chips - 1, 0, 1 + lax.rem(at + chips // 2 - 1, chips - 1))
    return lax.rem(row // 2 + way * dx + chips, chips) * 2 + lax.rem(row + 1 - same, 2)


def kernel(
    n_src, n_dst,
    edge_ref, atom_ref, targ_ref, rev_ref, cnt_ref, w_in_ref, gains_ref, w_lay_ref, w_rev_ref, w_down_ref, w_atom_ref,
    edge_out_ref, atom_out_ref,
    edges, xs, send, recv, atoms, proj, targ, rev, cnt, gains, w_in, w_lay, w_rev, w_down, w_atom, seg, part, parts,
    in_sem, w_sem, at_send, at_recv, send_sem, recv_sem, pt_send, pt_recv,
):
    planes = n_dst // PLANE
    width = edges.shape[1]
    layers = w_lay.shape[0]
    n_atoms = proj.shape[0]
    row = lax.axis_index("src")
    me = lax.axis_index("dst")
    z, y, c = me // PLANE, lax.rem(me // 2, 2), lax.rem(me, 2)

    barrier = pltpu.get_barrier_semaphore()

    @pl.loop(1, n_src)
    def _(d):
        pl.semaphore_signal(barrier, inc=1, device_id={"src": lax.rem(row + d, n_src)}, device_id_type=MESH)

    @pl.loop(1, n_dst)
    def _(d):
        pl.semaphore_signal(barrier, inc=1, device_id={"dst": lax.rem(me + d, n_dst)}, device_id_type=MESH)

    def partner(n, way):
        r, i = n // PLANE, lax.rem(n, PLANE)
        dz = planes // 2 * lax.rem(r + i, 2) + lax.rem(r // 2 + i + 1, planes // 2)
        py = lax.rem(y + i, 2)
        pc = lax.rem(c + (i + 1) // 2, 2)
        return lax.rem(z + way * dz + planes, planes) * PLANE + py * 2 + pc

    def rows_of(k):
        return pl.ds(pl.multiple_of(k * RB, RB), RB)

    def edge_load(k):
        return pltpu.make_async_copy(edge_ref.at[rows_of(k)], edges.at[rows_of(k)], in_sem.at[k])

    loads = [
        pltpu.make_async_copy(src, dst, w_sem.at[i])
        for i, (src, dst) in enumerate(
            [
                (atom_ref, atoms.at[row]), (w_in_ref, w_in), (targ_ref, targ), (gains_ref, gains), (w_lay_ref, w_lay),
                (rev_ref, rev), (w_rev_ref, w_rev), (cnt_ref, cnt), (w_down_ref, w_down), (w_atom_ref, w_atom),
            ]
        )
    ]
    for load in loads[:6]:
        load.start()

    @pl.loop(0, n_dst)
    def _(n):
        edge_load(partner(n, 1)).start()

    for load in loads[6:]:
        load.start()
    seg[...] = jnp.zeros_like(seg)
    loads[0].wait()
    pl.semaphore_wait(barrier, n_src + n_dst - 2)

    def atom_copy(d):
        return pltpu.make_async_remote_copy(
            src_ref=atoms.at[row], dst_ref=atoms.at[row], send_sem=at_send.at[d], recv_sem=at_recv.at[d],
            device_id={"src": far_peer(row, d, 1, n_src)}, device_id_type=MESH,
        )

    def atom_arrival(d):
        sender = far_peer(row, d, -1, n_src)
        return pltpu.make_async_remote_copy(
            src_ref=atoms.at[row], dst_ref=atoms.at[sender], send_sem=at_send.at[d], recv_sem=at_recv.at[d],
            device_id={"src": sender}, device_id_type=MESH,
        )

    @pl.loop(1, n_src)
    def _(d):
        atom_copy(d).start()

    for load in loads[1:6]:
        load.wait()

    @pl.loop(1, n_src)
    def _(d):
        atom_arrival(d).wait_recv()

    @pl.loop(1, n_src)
    def _(d):
        atom_copy(d).wait_send()

    whole = atoms[...].reshape(n_atoms, atoms.shape[2])
    proj[...] = jnp.dot(whole, w_in[...], preferred_element_type=jnp.float32).astype(jnp.bfloat16)

    def block_copy(k):
        return pltpu.make_async_remote_copy(
            src_ref=send.at[k], dst_ref=recv.at[me], send_sem=send_sem.at[k], recv_sem=recv_sem.at[me],
            device_id={"dst": k}, device_id_type=MESH,
        )

    def arrival(k):
        return pltpu.make_async_remote_copy(
            src_ref=send.at[k], dst_ref=recv.at[k], send_sem=send_sem.at[k], recv_sem=recv_sem.at[k],
            device_id={"dst": k}, device_id_type=MESH,
        )

    def own_copy():
        return pltpu.make_async_copy(send.at[me], recv.at[me], recv_sem.at[me])

    @pl.loop(0, n_dst // AHEAD)
    def _(step):
        ks = [partner(step * AHEAD + g, 1) for g in range(AHEAD)]
        hot, base = [], []
        for k in ks:
            edge_load(k).wait()
            base.append(edges[rows_of(k), :].astype(jnp.float32))
            col = jnp.broadcast_to(targ[k], (RB, RB)).T
            lane = lax.broadcasted_iota(jnp.int32, (RB, RB), 1)
            hot.append(
                jnp.concatenate(
                    [(col == lane + p * RB).astype(jnp.float32).astype(jnp.bfloat16) for p in range(n_atoms // RB)], axis=1
                )
            )
        picked = jnp.dot(jnp.concatenate(hot, axis=0), proj[...], preferred_element_type=jnp.float32)
        x = jnp.concatenate(base, axis=0) + picked
        for layer in range(layers):
            scale = lax.rsqrt(jnp.mean(x * x, axis=-1, keepdims=True) + 1e-6)
            normed = (x * scale * gains[layer : layer + 1, :]).astype(jnp.bfloat16)
            x = x + silu(jnp.dot(normed, w_lay[layer], preferred_element_type=jnp.float32))
        sent = x.astype(jnp.bfloat16)
        for g, k in enumerate(ks):
            xs[rows_of(k), :] = x[g * RB : (g + 1) * RB, :]
            sub = lax.broadcasted_iota(jnp.int32, (RB, RB), 0)
            perm = (sub == rev[k]).astype(jnp.float32).astype(jnp.bfloat16)
            moved = jnp.dot(perm, sent[g * RB : (g + 1) * RB, :], preferred_element_type=jnp.float32)
            send[k] = moved.astype(jnp.bfloat16)

            @pl.when(k != me)
            def _():
                block_copy(k).start()

            @pl.when(k == me)
            def _():
                own_copy().start()

    for load in loads[6:]:
        load.wait()

    @pl.loop(0, n_dst // BEHIND)
    def _(step):
        ks = [partner(step * BEHIND + g, -1) for g in range(BEHIND)]
        for k in ks:

            @pl.when(k != me)
            def _():
                arrival(k).wait_recv()

            @pl.when(k == me)
            def _():
                own_copy().wait()

        came = jnp.concatenate([recv[k] for k in ks], axis=0)
        message = jnp.dot(came, w_rev[...], preferred_element_type=jnp.float32)
        kept, hot = [], []
        for g, k in enumerate(ks):
            slot = lax.broadcasted_iota(jnp.int32, (RB, width), 0)
            total = xs[rows_of(k), :] + message[g * RB : (g + 1) * RB, :]
            result = jnp.where(slot < cnt[k], total, 0.0).astype(jnp.bfloat16)
            edge_out_ref[rows_of(k), :] = result
            kept.append(result)
            sub = lax.broadcasted_iota(jnp.int32, (n_atoms, RB), 0)
            hot.append((sub == targ[k]).astype(jnp.float32).astype(jnp.bfloat16))
        seg[...] += jnp.dot(
            jnp.concatenate(hot, axis=1), jnp.concatenate(kept, axis=0), preferred_element_type=jnp.float32
        )

    down = jnp.dot(seg[...].astype(jnp.bfloat16), w_down[...], preferred_element_type=jnp.float32)
    part[...] = down.astype(jnp.bfloat16).reshape(part.shape)

    def part_copy(d):
        to = far_peer(row, d, 1, n_src)
        return pltpu.make_async_remote_copy(
            src_ref=part.at[to], dst_ref=parts.at[d], send_sem=pt_send.at[d], recv_sem=pt_recv.at[d],
            device_id={"src": to}, device_id_type=MESH,
        )

    @pl.loop(1, n_src)
    def _(d):
        part_copy(d).start()

    agg = part[row].astype(jnp.float32)

    @pl.loop(1, n_src)
    def _(d):
        part_copy(d).wait()

    for d in range(1, n_src):
        agg = agg + parts[d].astype(jnp.float32)
    act = silu(0.3 * agg).astype(jnp.bfloat16)
    update = jnp.dot(act, w_atom[...], preferred_element_type=jnp.float32)
    atom_out_ref[...] = (atoms[row].astype(jnp.float32) + update).astype(jnp.bfloat16)

    @pl.loop(0, n_dst)
    def _(k):
        @pl.when(k != me)
        def _():
            arrival(k).wait_send()


def solution(mesh):
    n_src, n_dst = mesh.shape["src"], mesh.shape["dst"]

    def on_device(edge_in, atom_in, targets, reverse, counts, w_in, gains, w_layers, w_rev, w_down, w_atom):
        slots, width = edge_in.shape
        own, depth = atom_in.shape
        n_atoms = own * n_src
        bf16, f32 = jnp.bfloat16, jnp.float32
        hbm = pl.BlockSpec(memory_space=pltpu.HBM)
        vmem = pl.BlockSpec(memory_space=pltpu.VMEM)
        dma = pltpu.SemaphoreType.DMA
        return pl.pallas_call(
            functools.partial(kernel, n_src, n_dst),
            out_shape=(
                pltpu.VMEM(edge_in.shape, bf16),
                pltpu.VMEM(atom_in.shape, bf16),
            ),
            in_specs=[hbm] * 11,
            out_specs=(vmem, vmem),
            scratch_shapes=[
                pltpu.VMEM((slots, width), bf16),
                pltpu.VMEM((slots, width), f32),
                pltpu.VMEM((n_dst, RB, width), bf16),
                pltpu.VMEM((n_dst, RB, width), bf16),
                pltpu.VMEM((n_src, own, depth), bf16),
                pltpu.VMEM((n_atoms, width), bf16),
                pltpu.VMEM((n_dst, 1, RB), jnp.int32),
                pltpu.VMEM((n_dst, 1, RB), jnp.int32),
                pltpu.SMEM((n_dst,), jnp.int32),
                pltpu.VMEM(gains.shape, f32),
                pltpu.VMEM(w_in.shape, bf16),
                pltpu.VMEM(w_layers.shape, bf16),
                pltpu.VMEM(w_rev.shape, bf16),
                pltpu.VMEM(w_down.shape, bf16),
                pltpu.VMEM(w_atom.shape, bf16),
                pltpu.VMEM((n_atoms, width), f32),
                pltpu.VMEM((n_src, own, depth), bf16),
                pltpu.VMEM((n_src, own, depth), bf16),
                dma((n_dst,)),
                dma((10,)),
                dma((n_src,)),
                dma((n_src,)),
                dma((n_dst,)),
                dma((n_dst,)),
                dma((n_src,)),
                dma((n_src,)),
            ],
            compiler_params=pltpu.CompilerParams(
                collective_id=0, has_side_effects=True, vmem_limit_bytes=VMEM_MIB * 2**20
            ),
        )(
            edge_in, atom_in, targets.reshape(n_dst, 1, RB), reverse.reshape(n_dst, 1, RB), counts.reshape(n_dst),
            w_in, gains, w_layers, w_rev, w_down, w_atom,
        )

    both = ("src", "dst")
    in_specs = (
        P(both, None), P(("dst", "src"), None), P(both), P(both), P("src", "dst", None),
        P(), P(), P(), P(), P(), P(),
    )
    out_specs = (P(both, None), P(("dst", "src"), None))
    return jax.shard_map(on_device, mesh=mesh, in_specs=in_specs, out_specs=out_specs, check_vma=False)
```

```python
import functools

import jax
import jax.numpy as jnp
from jax import lax
from jax.experimental import pallas as pl
from jax.experimental.pallas import tpu as pltpu
from jax.sharding import PartitionSpec as P

MESH = pl.DeviceIdType.MESH
RB = 128
PLANE = 4
AHEAD = 2
BEHIND = 2
VMEM_MIB = 54
EARLY = (2, 4)


def silu(v):
    half = 0.5 * v
    return half + half * jnp.tanh(half)


def far_peer(row, d, way, n_src):
    chips = n_src // 2
    same = d // (chips + 1)
    at = d - 1 - same * chips
    dx = jnp.where(at == chips - 1, 0, 1 + lax.rem(at + chips // 2 - 1, chips - 1))
    return lax.rem(row // 2 + way * dx + chips, chips) * 2 + lax.rem(row + 1 - same, 2)


def kernel(
    n_src, n_dst,
    edge_ref, atom_ref, targ_ref, rev_ref, cnt_ref, w_in_ref, gains_ref, w_lay_ref, w_rev_ref, w_down_ref, w_atom_ref,
    edge_out_ref, atom_out_ref,
    edges, xs, send, recv, atoms, proj, targ, rev, cnt, gains, w_in, w_lay, w_rev, w_down, w_atom, seg, part, parts,
    rows_send, rows_recv,
    in_sem, w_sem, at_send, at_recv, send_sem, recv_sem, pt_send, pt_recv, rw_send, rw_recv,
):
    planes = n_dst // PLANE
    width = edges.shape[1]
    layers = w_lay.shape[0]
    n_atoms = proj.shape[0]
    row = lax.axis_index("src")
    me = lax.axis_index("dst")
    z, y, c = me // PLANE, lax.rem(me // 2, 2), lax.rem(me, 2)

    barrier = pltpu.get_barrier_semaphore()

    @pl.loop(1, n_src)
    def _(d):
        pl.semaphore_signal(barrier, inc=1, device_id={"src": lax.rem(row + d, n_src)}, device_id_type=MESH)

    @pl.loop(1, n_dst)
    def _(d):
        pl.semaphore_signal(barrier, inc=1, device_id={"dst": lax.rem(me + d, n_dst)}, device_id_type=MESH)

    def partner(n, way):
        r, i = n // PLANE, lax.rem(n, PLANE)
        dz = planes // 2 * lax.rem(r + i, 2) + lax.rem(r // 2 + i + 1, planes // 2)
        py = lax.rem(y + i, 2)
        pc = lax.rem(c + (i + 1) // 2, 2)
        return lax.rem(z + way * dz + planes, planes) * PLANE + py * 2 + pc

    def rows_of(k):
        return pl.ds(pl.multiple_of(k * RB, RB), RB)

    def edge_load(k):
        return pltpu.make_async_copy(edge_ref.at[rows_of(k)], edges.at[rows_of(k)], in_sem.at[k])

    loads = [
        pltpu.make_async_copy(src, dst, w_sem.at[i])
        for i, (src, dst) in enumerate(
            [
                (atom_ref, atoms.at[row]), (w_in_ref, w_in), (targ_ref, targ), (gains_ref, gains), (w_lay_ref, w_lay),
                (rev_ref, rev), (w_rev_ref, w_rev), (cnt_ref, cnt), (w_down_ref, w_down), (w_atom_ref, w_atom),
            ]
        )
    ]
    for load in loads[:6]:
        load.start()

    @pl.loop(0, n_dst)
    def _(n):
        edge_load(partner(n, 1)).start()

    for load in loads[6:]:
        load.start()
    seg[...] = jnp.zeros_like(seg)
    loads[0].wait()
    pl.semaphore_wait(barrier, n_src + n_dst - 2)

    def block_copy(k):
        return pltpu.make_async_remote_copy(
            src_ref=send.at[k], dst_ref=recv.at[me], send_sem=send_sem.at[k], recv_sem=recv_sem.at[me],
            device_id={"dst": k}, device_id_type=MESH,
        )

    def arrival(k):
        return pltpu.make_async_remote_copy(
            src_ref=send.at[k], dst_ref=recv.at[k], send_sem=send_sem.at[k], recv_sem=recv_sem.at[k],
            device_id={"dst": k}, device_id_type=MESH,
        )

    def own_copy():
        return pltpu.make_async_copy(send.at[me], recv.at[me], recv_sem.at[me])

    def rows_copy(s):
        return pltpu.make_async_remote_copy(
            src_ref=rows_send.at[s], dst_ref=rows_recv.at[s], send_sem=rw_send.at[s], recv_sem=rw_recv.at[s],
            device_id={"dst": partner(EARLY[s], 1)}, device_id_type=MESH,
        )

    def early(n):
        return functools.reduce(jnp.logical_or, [n == e for e in EARLY])

    def reorder(k):
        sub = lax.broadcasted_iota(jnp.int32, (RB, RB), 0)
        return (sub == rev[k]).astype(jnp.float32).astype(jnp.bfloat16)

    def edge_layers(x):
        for layer in range(layers):
            scale = lax.rsqrt(jnp.mean(x * x, axis=-1, keepdims=True) + 1e-6)
            normed = (x * scale * gains[layer : layer + 1, :]).astype(jnp.bfloat16)
            x = x + silu(jnp.dot(normed, w_lay[layer], preferred_element_type=jnp.float32))
        return x

    def atom_copy(d):
        return pltpu.make_async_remote_copy(
            src_ref=atoms.at[row], dst_ref=atoms.at[row], send_sem=at_send.at[d], recv_sem=at_recv.at[d],
            device_id={"src": far_peer(row, d, 1, n_src)}, device_id_type=MESH,
        )

    def atom_arrival(d):
        sender = far_peer(row, d, -1, n_src)
        return pltpu.make_async_remote_copy(
            src_ref=atoms.at[row], dst_ref=atoms.at[sender], send_sem=at_send.at[d], recv_sem=at_recv.at[d],
            device_id={"src": sender}, device_id_type=MESH,
        )

    @pl.loop(1, n_src)
    def _(d):
        atom_copy(d).start()

    for load in loads[1:6]:
        load.wait()

    for n in EARLY:
        k = partner(n, 1)
        edge_load(k).wait()
        moved = jnp.dot(reorder(k), edges[rows_of(k), :], preferred_element_type=jnp.float32)
        send[k] = moved.astype(jnp.bfloat16)
        block_copy(k).start()

    @pl.loop(1, n_src)
    def _(d):
        atom_arrival(d).wait_recv()

    @pl.loop(1, n_src)
    def _(d):
        atom_copy(d).wait_send()

    def every_atom():
        return atoms[...].reshape(n_atoms, atoms.shape[2])

    proj[...] = jnp.dot(every_atom(), w_in[...], preferred_element_type=jnp.float32).astype(jnp.bfloat16)

    @pl.loop(0, n_dst // AHEAD)
    def _(step):
        ns = [step * AHEAD + g for g in range(AHEAD)]
        ks = [partner(n, 1) for n in ns]
        hot, base = [], []
        for n, k in zip(ns, ks):

            @pl.when(jnp.logical_not(early(n)))
            def _():
                edge_load(k).wait()

            base.append(edges[rows_of(k), :].astype(jnp.float32))
            col = jnp.broadcast_to(targ[k], (RB, RB)).T
            lane = lax.broadcasted_iota(jnp.int32, (RB, RB), 1)
            hot.append(
                jnp.concatenate(
                    [(col == lane + p * RB).astype(jnp.float32).astype(jnp.bfloat16) for p in range(n_atoms // RB)], axis=1
                )
            )
        picked = jnp.dot(jnp.concatenate(hot, axis=0), proj[...], preferred_element_type=jnp.float32)
        x = edge_layers(jnp.concatenate(base, axis=0) + picked)
        sent = x.astype(jnp.bfloat16)
        for g, (n, k) in enumerate(zip(ns, ks)):
            xs[rows_of(k), :] = x[g * RB : (g + 1) * RB, :]
            perm = reorder(k)

            def whole_rows():
                moved = jnp.dot(perm, sent[g * RB : (g + 1) * RB, :], preferred_element_type=jnp.float32)
                send[k] = moved.astype(jnp.bfloat16)

                @pl.when(k != me)
                def _():
                    block_copy(k).start()

                @pl.when(k == me)
                def _():
                    own_copy().start()

            def atom_rows(s):
                rows = jnp.dot(hot[g], every_atom(), preferred_element_type=jnp.float32).astype(jnp.bfloat16)
                rows_send[s] = jnp.dot(perm, rows, preferred_element_type=jnp.float32).astype(jnp.bfloat16)
                rows_copy(s).start()

            pl.when(jnp.logical_not(early(n)))(whole_rows)
            for s, e in enumerate(EARLY):
                if e % AHEAD == g:
                    pl.when(n == e)(functools.partial(atom_rows, s))

    for load in loads[6:]:
        load.wait()

    begun = []
    for s, n in enumerate(EARLY):
        k = partner(n, -1)
        arrival(k).wait_recv()
        rows_copy(s).wait_recv()
        near = jnp.dot(rows_recv[s], w_in[...], preferred_element_type=jnp.float32).astype(jnp.bfloat16)
        begun.append(recv[k].astype(jnp.float32) + near.astype(jnp.float32))
    states = edge_layers(jnp.concatenate(begun, axis=0)).astype(jnp.bfloat16)
    for s, n in enumerate(EARLY):
        recv[partner(n, -1)] = states[s * RB : (s + 1) * RB, :]

    @pl.loop(0, n_dst // BEHIND)
    def _(step):
        ns = [step * BEHIND + g for g in range(BEHIND)]
        ks = [partner(n, -1) for n in ns]
        for n, k in zip(ns, ks):

            @pl.when((k != me) & jnp.logical_not(early(n)))
            def _():
                arrival(k).wait_recv()

            @pl.when(k == me)
            def _():
                own_copy().wait()

        came = jnp.concatenate([recv[k] for k in ks], axis=0)
        message = jnp.dot(came, w_rev[...], preferred_element_type=jnp.float32)
        kept, hot = [], []
        for g, k in enumerate(ks):
            slot = lax.broadcasted_iota(jnp.int32, (RB, width), 0)
            total = xs[rows_of(k), :] + message[g * RB : (g + 1) * RB, :]
            result = jnp.where(slot < cnt[k], total, 0.0).astype(jnp.bfloat16)
            edge_out_ref[rows_of(k), :] = result
            kept.append(result)
            sub = lax.broadcasted_iota(jnp.int32, (n_atoms, RB), 0)
            hot.append((sub == targ[k]).astype(jnp.float32).astype(jnp.bfloat16))
        seg[...] += jnp.dot(
            jnp.concatenate(hot, axis=1), jnp.concatenate(kept, axis=0), preferred_element_type=jnp.float32
        )

    down = jnp.dot(seg[...].astype(jnp.bfloat16), w_down[...], preferred_element_type=jnp.float32)
    part[...] = down.astype(jnp.bfloat16).reshape(part.shape)

    def part_copy(d):
        to = far_peer(row, d, 1, n_src)
        return pltpu.make_async_remote_copy(
            src_ref=part.at[to], dst_ref=parts.at[d], send_sem=pt_send.at[d], recv_sem=pt_recv.at[d],
            device_id={"src": to}, device_id_type=MESH,
        )

    @pl.loop(1, n_src)
    def _(d):
        part_copy(d).start()

    agg = part[row].astype(jnp.float32)

    @pl.loop(1, n_src)
    def _(d):
        part_copy(d).wait()

    for d in range(1, n_src):
        agg = agg + parts[d].astype(jnp.float32)
    act = silu(0.3 * agg).astype(jnp.bfloat16)
    update = jnp.dot(act, w_atom[...], preferred_element_type=jnp.float32)
    atom_out_ref[...] = (atoms[row].astype(jnp.float32) + update).astype(jnp.bfloat16)

    @pl.loop(0, n_dst)
    def _(k):
        @pl.when(k != me)
        def _():
            arrival(k).wait_send()

    for s in range(len(EARLY)):
        rows_copy(s).wait_send()


def solution(mesh):
    n_src, n_dst = mesh.shape["src"], mesh.shape["dst"]

    def on_device(edge_in, atom_in, targets, reverse, counts, w_in, gains, w_layers, w_rev, w_down, w_atom):
        slots, width = edge_in.shape
        own, depth = atom_in.shape
        n_atoms = own * n_src
        bf16, f32 = jnp.bfloat16, jnp.float32
        hbm = pl.BlockSpec(memory_space=pltpu.HBM)
        vmem = pl.BlockSpec(memory_space=pltpu.VMEM)
        dma = pltpu.SemaphoreType.DMA
        return pl.pallas_call(
            functools.partial(kernel, n_src, n_dst),
            out_shape=(
                pltpu.VMEM(edge_in.shape, bf16),
                pltpu.VMEM(atom_in.shape, bf16),
            ),
            in_specs=[hbm] * 11,
            out_specs=(vmem, vmem),
            scratch_shapes=[
                pltpu.VMEM((slots, width), bf16),
                pltpu.VMEM((slots, width), f32),
                pltpu.VMEM((n_dst, RB, width), bf16),
                pltpu.VMEM((n_dst, RB, width), bf16),
                pltpu.VMEM((n_src, own, depth), bf16),
                pltpu.VMEM((n_atoms, width), bf16),
                pltpu.VMEM((n_dst, 1, RB), jnp.int32),
                pltpu.VMEM((n_dst, 1, RB), jnp.int32),
                pltpu.SMEM((n_dst,), jnp.int32),
                pltpu.VMEM(gains.shape, f32),
                pltpu.VMEM(w_in.shape, bf16),
                pltpu.VMEM(w_layers.shape, bf16),
                pltpu.VMEM(w_rev.shape, bf16),
                pltpu.VMEM(w_down.shape, bf16),
                pltpu.VMEM(w_atom.shape, bf16),
                pltpu.VMEM((n_atoms, width), f32),
                pltpu.VMEM((n_src, own, depth), bf16),
                pltpu.VMEM((n_src, own, depth), bf16),
                pltpu.VMEM((len(EARLY), RB, depth), bf16),
                pltpu.VMEM((len(EARLY), RB, depth), bf16),
                dma((n_dst,)),
                dma((10,)),
                dma((n_src,)),
                dma((n_src,)),
                dma((n_dst,)),
                dma((n_dst,)),
                dma((n_src,)),
                dma((n_src,)),
                dma((len(EARLY),)),
                dma((len(EARLY),)),
            ],
            compiler_params=pltpu.CompilerParams(
                collective_id=0, has_side_effects=True, vmem_limit_bytes=VMEM_MIB * 2**20
            ),
        )(
            edge_in, atom_in, targets.reshape(n_dst, 1, RB), reverse.reshape(n_dst, 1, RB), counts.reshape(n_dst),
            w_in, gains, w_layers, w_rev, w_down, w_atom,
        )

    both = ("src", "dst")
    in_specs = (
        P(both, None), P(("dst", "src"), None), P(both), P(both), P("src", "dst", None),
        P(), P(), P(), P(), P(), P(),
    )
    out_specs = (P(both, None), P(("dst", "src"), None))
    return jax.shard_map(on_device, mesh=mesh, in_specs=in_specs, out_specs=out_specs, check_vma=False)
```

```python
import functools

import jax
import jax.numpy as jnp
from jax import lax
from jax.experimental import pallas as pl
from jax.experimental.pallas import tpu as pltpu
from jax.sharding import PartitionSpec as P

MESH = pl.DeviceIdType.MESH
RB = 128
PLANE = 4
AHEAD = 2
BEHIND = 2
VMEM_MIB = 54
EARLY = (2, 4)


def silu(v):
    half = 0.5 * v
    return half + half * jnp.tanh(half)


def far_peer(row, d, way, n_src):
    chips = n_src // 2
    same = d // (chips + 1)
    at = d - 1 - same * chips
    dx = jnp.where(at == chips - 1, 0, 1 + lax.rem(at + chips // 2 - 1, chips - 1))
    return lax.rem(row // 2 + way * dx + chips, chips) * 2 + lax.rem(row + 1 - same, 2)


def kernel(
    n_src, n_dst,
    edge_ref, atom_ref, targ_ref, rev_ref, cnt_ref, w_in_ref, gains_ref, w_lay_ref, w_rev_ref, w_down_ref, w_atom_ref,
    edge_out_ref, atom_out_ref,
    edges, xs, send, recv, atoms, proj, targ, rev, cnt, gains, w_in, w_lay, w_rev, w_down, w_atom, seg, part, parts,
    rows_send, rows_recv,
    in_sem, w_sem, at_send, at_recv, send_sem, recv_sem, pt_send, pt_recv, rw_send, rw_recv,
):
    planes = n_dst // PLANE
    width = edges.shape[1]
    layers = w_lay.shape[0]
    n_atoms = proj.shape[0]
    row = lax.axis_index("src")
    me = lax.axis_index("dst")
    z, y, c = me // PLANE, lax.rem(me // 2, 2), lax.rem(me, 2)

    barrier = pltpu.get_barrier_semaphore()

    @pl.loop(1, n_src)
    def _(d):
        pl.semaphore_signal(barrier, inc=1, device_id={"src": lax.rem(row + d, n_src)}, device_id_type=MESH)

    @pl.loop(1, n_dst)
    def _(d):
        pl.semaphore_signal(barrier, inc=1, device_id={"dst": lax.rem(me + d, n_dst)}, device_id_type=MESH)

    def partner(n, way):
        r, i = n // PLANE, lax.rem(n, PLANE)
        r = jnp.where(r >= planes - 2, 2 * planes - 3 - r, r)
        dz = planes // 2 * lax.rem(r + i, 2) + lax.rem(r // 2 + i + 1, planes // 2)
        py = lax.rem(y + i, 2)
        pc = lax.rem(c + (i + 1) // 2, 2)
        return lax.rem(z + way * dz + planes, planes) * PLANE + py * 2 + pc

    def rows_of(k):
        return pl.ds(pl.multiple_of(k * RB, RB), RB)

    def edge_load(k):
        return pltpu.make_async_copy(edge_ref.at[rows_of(k)], edges.at[rows_of(k)], in_sem.at[k])

    loads = [
        pltpu.make_async_copy(src, dst, w_sem.at[i])
        for i, (src, dst) in enumerate(
            [
                (atom_ref, atoms.at[row]), (w_in_ref, w_in), (targ_ref, targ), (gains_ref, gains), (w_lay_ref, w_lay),
                (rev_ref, rev), (w_rev_ref, w_rev), (cnt_ref, cnt), (w_down_ref, w_down), (w_atom_ref, w_atom),
            ]
        )
    ]
    for load in loads[:6]:
        load.start()

    @pl.loop(0, n_dst)
    def _(n):
        edge_load(partner(n, 1)).start()

    for load in loads[6:]:
        load.start()
    seg[...] = jnp.zeros_like(seg)

    def reorder(k):
        sub = lax.broadcasted_iota(jnp.int32, (RB, RB), 0)
        return (sub == rev[k]).astype(jnp.float32).astype(jnp.bfloat16)

    for load in loads[1:6]:
        load.wait()
    for n in EARLY:
        k = partner(n, 1)
        edge_load(k).wait()
        moved = jnp.dot(reorder(k), edges[rows_of(k), :], preferred_element_type=jnp.float32)
        send[k] = moved.astype(jnp.bfloat16)

    loads[0].wait()
    pl.semaphore_wait(barrier, n_src + n_dst - 2)

    def block_copy(k):
        return pltpu.make_async_remote_copy(
            src_ref=send.at[k], dst_ref=recv.at[me], send_sem=send_sem.at[k], recv_sem=recv_sem.at[me],
            device_id={"dst": k}, device_id_type=MESH,
        )

    def arrival(k):
        return pltpu.make_async_remote_copy(
            src_ref=send.at[k], dst_ref=recv.at[k], send_sem=send_sem.at[k], recv_sem=recv_sem.at[k],
            device_id={"dst": k}, device_id_type=MESH,
        )

    def own_copy():
        return pltpu.make_async_copy(send.at[me], recv.at[me], recv_sem.at[me])

    def rows_copy(s):
        return pltpu.make_async_remote_copy(
            src_ref=rows_send.at[s], dst_ref=rows_recv.at[s], send_sem=rw_send.at[s], recv_sem=rw_recv.at[s],
            device_id={"dst": partner(EARLY[s], 1)}, device_id_type=MESH,
        )

    def early(n):
        return functools.reduce(jnp.logical_or, [n == e for e in EARLY])

    def edge_layers(x):
        for layer in range(layers):
            scale = lax.rsqrt(jnp.mean(x * x, axis=-1, keepdims=True) + 1e-6)
            normed = (x * scale * gains[layer : layer + 1, :]).astype(jnp.bfloat16)
            x = x + silu(jnp.dot(normed, w_lay[layer], preferred_element_type=jnp.float32))
        return x

    def atom_copy(d):
        return pltpu.make_async_remote_copy(
            src_ref=atoms.at[row], dst_ref=atoms.at[row], send_sem=at_send.at[d], recv_sem=at_recv.at[d],
            device_id={"src": far_peer(row, d, 1, n_src)}, device_id_type=MESH,
        )

    def atom_arrival(d):
        sender = far_peer(row, d, -1, n_src)
        return pltpu.make_async_remote_copy(
            src_ref=atoms.at[row], dst_ref=atoms.at[sender], send_sem=at_send.at[d], recv_sem=at_recv.at[d],
            device_id={"src": sender}, device_id_type=MESH,
        )

    for n in EARLY:
        block_copy(partner(n, 1)).start()

    @pl.loop(1, n_src)
    def _(d):
        atom_copy(d).start()

    @pl.loop(1, n_src)
    def _(d):
        atom_arrival(d).wait_recv()

    @pl.loop(1, n_src)
    def _(d):
        atom_copy(d).wait_send()

    def every_atom():
        return atoms[...].reshape(n_atoms, atoms.shape[2])

    proj[...] = jnp.dot(every_atom(), w_in[...], preferred_element_type=jnp.float32).astype(jnp.bfloat16)

    @pl.loop(0, n_dst // AHEAD)
    def _(step):
        ns = [step * AHEAD + g for g in range(AHEAD)]
        ks = [partner(n, 1) for n in ns]
        hot, base = [], []
        for n, k in zip(ns, ks):

            @pl.when(jnp.logical_not(early(n)))
            def _():
                edge_load(k).wait()

            base.append(edges[rows_of(k), :].astype(jnp.float32))
            col = jnp.broadcast_to(targ[k], (RB, RB)).T
            lane = lax.broadcasted_iota(jnp.int32, (RB, RB), 1)
            hot.append(
                jnp.concatenate(
                    [(col == lane + p * RB).astype(jnp.float32).astype(jnp.bfloat16) for p in range(n_atoms // RB)], axis=1
                )
            )
        picked = jnp.dot(jnp.concatenate(hot, axis=0), proj[...], preferred_element_type=jnp.float32)
        x = edge_layers(jnp.concatenate(base, axis=0) + picked)
        sent = x.astype(jnp.bfloat16)
        for g, (n, k) in enumerate(zip(ns, ks)):
            xs[rows_of(k), :] = x[g * RB : (g + 1) * RB, :]
            perm = reorder(k)

            def whole_rows():
                moved = jnp.dot(perm, sent[g * RB : (g + 1) * RB, :], preferred_element_type=jnp.float32)
                send[k] = moved.astype(jnp.bfloat16)

                @pl.when(k != me)
                def _():
                    block_copy(k).start()

                @pl.when(k == me)
                def _():
                    own_copy().start()

            def atom_rows(s):
                rows = jnp.dot(hot[g], every_atom(), preferred_element_type=jnp.float32).astype(jnp.bfloat16)
                rows_send[s] = jnp.dot(perm, rows, preferred_element_type=jnp.float32).astype(jnp.bfloat16)
                rows_copy(s).start()

            pl.when(jnp.logical_not(early(n)))(whole_rows)
            for s, e in enumerate(EARLY):
                if e % AHEAD == g:
                    pl.when(n == e)(functools.partial(atom_rows, s))

    for load in loads[6:]:
        load.wait()

    begun = []
    for s, n in enumerate(EARLY):
        k = partner(n, -1)
        arrival(k).wait_recv()
        rows_copy(s).wait_recv()
        near = jnp.dot(rows_recv[s], w_in[...], preferred_element_type=jnp.float32).astype(jnp.bfloat16)
        begun.append(recv[k].astype(jnp.float32) + near.astype(jnp.float32))
    states = edge_layers(jnp.concatenate(begun, axis=0)).astype(jnp.bfloat16)
    for s, n in enumerate(EARLY):
        recv[partner(n, -1)] = states[s * RB : (s + 1) * RB, :]

    @pl.loop(0, n_dst // BEHIND)
    def _(step):
        ns = [step * BEHIND + g for g in range(BEHIND)]
        ks = [partner(n, -1) for n in ns]
        for n, k in zip(ns, ks):

            @pl.when((k != me) & jnp.logical_not(early(n)))
            def _():
                arrival(k).wait_recv()

            @pl.when(k == me)
            def _():
                own_copy().wait()

        came = jnp.concatenate([recv[k] for k in ks], axis=0)
        message = jnp.dot(came, w_rev[...], preferred_element_type=jnp.float32)
        kept, hot = [], []
        for g, k in enumerate(ks):
            slot = lax.broadcasted_iota(jnp.int32, (RB, width), 0)
            total = xs[rows_of(k), :] + message[g * RB : (g + 1) * RB, :]
            result = jnp.where(slot < cnt[k], total, 0.0).astype(jnp.bfloat16)
            edge_out_ref[rows_of(k), :] = result
            kept.append(result)
            sub = lax.broadcasted_iota(jnp.int32, (n_atoms, RB), 0)
            hot.append((sub == targ[k]).astype(jnp.float32).astype(jnp.bfloat16))
        seg[...] += jnp.dot(
            jnp.concatenate(hot, axis=1), jnp.concatenate(kept, axis=0), preferred_element_type=jnp.float32
        )

    down = jnp.dot(seg[...].astype(jnp.bfloat16), w_down[...], preferred_element_type=jnp.float32)
    part[...] = down.astype(jnp.bfloat16).reshape(part.shape)

    def part_copy(d):
        to = far_peer(row, d, 1, n_src)
        return pltpu.make_async_remote_copy(
            src_ref=part.at[to], dst_ref=parts.at[d], send_sem=pt_send.at[d], recv_sem=pt_recv.at[d],
            device_id={"src": to}, device_id_type=MESH,
        )

    @pl.loop(1, n_src)
    def _(d):
        part_copy(d).start()

    agg = part[row].astype(jnp.float32)

    @pl.loop(1, n_src)
    def _(d):
        part_copy(d).wait()

    for d in range(1, n_src):
        agg = agg + parts[d].astype(jnp.float32)
    act = silu(0.3 * agg).astype(jnp.bfloat16)
    update = jnp.dot(act, w_atom[...], preferred_element_type=jnp.float32)
    atom_out_ref[...] = (atoms[row].astype(jnp.float32) + update).astype(jnp.bfloat16)

    @pl.loop(0, n_dst)
    def _(k):
        @pl.when(k != me)
        def _():
            arrival(k).wait_send()

    for s in range(len(EARLY)):
        rows_copy(s).wait_send()


def solution(mesh):
    n_src, n_dst = mesh.shape["src"], mesh.shape["dst"]

    def on_device(edge_in, atom_in, targets, reverse, counts, w_in, gains, w_layers, w_rev, w_down, w_atom):
        slots, width = edge_in.shape
        own, depth = atom_in.shape
        n_atoms = own * n_src
        bf16, f32 = jnp.bfloat16, jnp.float32
        hbm = pl.BlockSpec(memory_space=pltpu.HBM)
        vmem = pl.BlockSpec(memory_space=pltpu.VMEM)
        dma = pltpu.SemaphoreType.DMA
        return pl.pallas_call(
            functools.partial(kernel, n_src, n_dst),
            out_shape=(
                pltpu.VMEM(edge_in.shape, bf16),
                pltpu.VMEM(atom_in.shape, bf16),
            ),
            in_specs=[hbm] * 11,
            out_specs=(vmem, vmem),
            scratch_shapes=[
                pltpu.VMEM((slots, width), bf16),
                pltpu.VMEM((slots, width), f32),
                pltpu.VMEM((n_dst, RB, width), bf16),
                pltpu.VMEM((n_dst, RB, width), bf16),
                pltpu.VMEM((n_src, own, depth), bf16),
                pltpu.VMEM((n_atoms, width), bf16),
                pltpu.VMEM((n_dst, 1, RB), jnp.int32),
                pltpu.VMEM((n_dst, 1, RB), jnp.int32),
                pltpu.SMEM((n_dst,), jnp.int32),
                pltpu.VMEM(gains.shape, f32),
                pltpu.VMEM(w_in.shape, bf16),
                pltpu.VMEM(w_layers.shape, bf16),
                pltpu.VMEM(w_rev.shape, bf16),
                pltpu.VMEM(w_down.shape, bf16),
                pltpu.VMEM(w_atom.shape, bf16),
                pltpu.VMEM((n_atoms, width), f32),
                pltpu.VMEM((n_src, own, depth), bf16),
                pltpu.VMEM((n_src, own, depth), bf16),
                pltpu.VMEM((len(EARLY), RB, depth), bf16),
                pltpu.VMEM((len(EARLY), RB, depth), bf16),
                dma((n_dst,)),
                dma((10,)),
                dma((n_src,)),
                dma((n_src,)),
                dma((n_dst,)),
                dma((n_dst,)),
                dma((n_src,)),
                dma((n_src,)),
                dma((len(EARLY),)),
                dma((len(EARLY),)),
            ],
            compiler_params=pltpu.CompilerParams(
                collective_id=0, has_side_effects=True, vmem_limit_bytes=VMEM_MIB * 2**20
            ),
        )(
            edge_in, atom_in, targets.reshape(n_dst, 1, RB), reverse.reshape(n_dst, 1, RB), counts.reshape(n_dst),
            w_in, gains, w_layers, w_rev, w_down, w_atom,
        )

    both = ("src", "dst")
    in_specs = (
        P(both, None), P(("dst", "src"), None), P(both), P(both), P("src", "dst", None),
        P(), P(), P(), P(), P(), P(),
    )
    out_specs = (P(both, None), P(("dst", "src"), None))
    return jax.shard_map(on_device, mesh=mesh, in_specs=in_specs, out_specs=out_specs, check_vma=False)
```

```python
import functools

import jax
import jax.numpy as jnp
from jax import lax
from jax.experimental import pallas as pl
from jax.experimental.pallas import tpu as pltpu
from jax.sharding import PartitionSpec as P

MESH = pl.DeviceIdType.MESH
RB = 128
PLANE = 4
AHEAD = 2
BEHIND = 2
VMEM_MIB = 54
EARLY = (2, 4)


def silu(v):
    half = 0.5 * v
    return half + half * jnp.tanh(half)


def far_peer(row, d, way, n_src):
    chips = n_src // 2
    same = d // (chips + 1)
    at = d - 1 - same * chips
    dx = jnp.where(at == chips - 1, 0, 1 + lax.rem(at + chips // 2 - 1, chips - 1))
    return lax.rem(row // 2 + way * dx + chips, chips) * 2 + lax.rem(row + 1 - same, 2)


def kernel(
    n_src, n_dst,
    edge_ref, atom_ref, targ_ref, rev_ref, cnt_ref, w_in_ref, gains_ref, w_lay_ref, w_rev_ref, w_down_ref, w_atom_ref,
    edge_out_ref, atom_out_ref,
    edges, xs, send, recv, atoms, proj, targ, rev, cnt, gains, w_in, w_lay, w_rev, w_down, w_atom, seg, part, parts,
    rows_send, rows_recv,
    in_sem, w_sem, at_send, at_recv, send_sem, recv_sem, pt_send, pt_recv, rw_send, rw_recv,
):
    planes = n_dst // PLANE
    width = edges.shape[1]
    layers = w_lay.shape[0]
    n_atoms = proj.shape[0]
    row = lax.axis_index("src")
    me = lax.axis_index("dst")
    z, y, c = me // PLANE, lax.rem(me // 2, 2), lax.rem(me, 2)

    barrier = pltpu.get_barrier_semaphore()

    @pl.loop(1, n_src)
    def _(d):
        pl.semaphore_signal(barrier, inc=1, device_id={"src": lax.rem(row + d, n_src)}, device_id_type=MESH)

    @pl.loop(1, n_dst)
    def _(d):
        pl.semaphore_signal(barrier, inc=1, device_id={"dst": lax.rem(me + d, n_dst)}, device_id_type=MESH)

    def partner(n, way):
        r, i = n // PLANE, lax.rem(n, PLANE)
        r = jnp.where(r >= planes - 2, 2 * planes - 3 - r, r)
        dz = planes // 2 * lax.rem(r + i, 2) + lax.rem(r // 2 + i + 1, planes // 2)
        py = lax.rem(y + i, 2)
        pc = lax.rem(c + (i + 1) // 2, 2)
        return lax.rem(z + way * dz + planes, planes) * PLANE + py * 2 + pc

    def rows_of(k):
        return pl.ds(pl.multiple_of(k * RB, RB), RB)

    def edge_load(k):
        return pltpu.make_async_copy(edge_ref.at[rows_of(k)], edges.at[rows_of(k)], in_sem.at[k])

    loads = [
        pltpu.make_async_copy(src, dst, w_sem.at[i])
        for i, (src, dst) in enumerate(
            [
                (atom_ref, atoms.at[row]), (w_in_ref, w_in), (targ_ref, targ), (gains_ref, gains), (w_lay_ref, w_lay),
                (rev_ref, rev), (w_rev_ref, w_rev), (cnt_ref, cnt), (w_down_ref, w_down), (w_atom_ref, w_atom),
            ]
        )
    ]
    for load in loads[:6]:
        load.start()

    @pl.loop(0, n_dst)
    def _(n):
        edge_load(partner(n, 1)).start()

    for load in loads[6:]:
        load.start()
    seg[...] = jnp.zeros_like(seg)
    loads[0].wait()
    pl.semaphore_wait(barrier, n_src + n_dst - 2)

    def block_copy(k):
        return pltpu.make_async_remote_copy(
            src_ref=send.at[k], dst_ref=recv.at[me], send_sem=send_sem.at[k], recv_sem=recv_sem.at[me],
            device_id={"dst": k}, device_id_type=MESH,
        )

    def arrival(k):
        return pltpu.make_async_remote_copy(
            src_ref=send.at[k], dst_ref=recv.at[k], send_sem=send_sem.at[k], recv_sem=recv_sem.at[k],
            device_id={"dst": k}, device_id_type=MESH,
        )

    def own_copy():
        return pltpu.make_async_copy(send.at[me], recv.at[me], recv_sem.at[me])

    def rows_copy(s):
        return pltpu.make_async_remote_copy(
            src_ref=rows_send.at[s], dst_ref=rows_recv.at[s], send_sem=rw_send.at[s], recv_sem=rw_recv.at[s],
            device_id={"dst": partner(EARLY[s], 1)}, device_id_type=MESH,
        )

    def early(n):
        return functools.reduce(jnp.logical_or, [n == e for e in EARLY])

    def reorder(k):
        sub = lax.broadcasted_iota(jnp.int32, (RB, RB), 0)
        return (sub == rev[k]).astype(jnp.float32).astype(jnp.bfloat16)

    def edge_layers(x):
        for layer in range(layers):
            scale = lax.rsqrt(jnp.mean(x * x, axis=-1, keepdims=True) + 1e-6)
            normed = (x * scale * gains[layer : layer + 1, :]).astype(jnp.bfloat16)
            x = x + silu(jnp.dot(normed, w_lay[layer], preferred_element_type=jnp.float32))
        return x

    def atom_copy(d):
        return pltpu.make_async_remote_copy(
            src_ref=atoms.at[row], dst_ref=atoms.at[row], send_sem=at_send.at[d], recv_sem=at_recv.at[d],
            device_id={"src": far_peer(row, d, 1, n_src)}, device_id_type=MESH,
        )

    def atom_arrival(d):
        sender = far_peer(row, d, -1, n_src)
        return pltpu.make_async_remote_copy(
            src_ref=atoms.at[row], dst_ref=atoms.at[sender], send_sem=at_send.at[d], recv_sem=at_recv.at[d],
            device_id={"src": sender}, device_id_type=MESH,
        )

    @pl.loop(1, n_src)
    def _(d):
        atom_copy(d).start()

    for load in loads[1:6]:
        load.wait()

    for n in EARLY:
        k = partner(n, 1)
        edge_load(k).wait()
        moved = jnp.dot(reorder(k), edges[rows_of(k), :], preferred_element_type=jnp.float32)
        send[k] = moved.astype(jnp.bfloat16)
        block_copy(k).start()

    @pl.loop(1, n_src)
    def _(d):
        atom_arrival(d).wait_recv()

    @pl.loop(1, n_src)
    def _(d):
        atom_copy(d).wait_send()

    def every_atom():
        return atoms[...].reshape(n_atoms, atoms.shape[2])

    proj[...] = jnp.dot(every_atom(), w_in[...], preferred_element_type=jnp.float32).astype(jnp.bfloat16)

    @pl.loop(0, n_dst // AHEAD)
    def _(step):
        ns = [step * AHEAD + g for g in range(AHEAD)]
        ks = [partner(n, 1) for n in ns]
        hot, base = [], []
        for n, k in zip(ns, ks):

            @pl.when(jnp.logical_not(early(n)))
            def _():
                edge_load(k).wait()

            base.append(edges[rows_of(k), :].astype(jnp.float32))
            col = jnp.broadcast_to(targ[k], (RB, RB)).T
            lane = lax.broadcasted_iota(jnp.int32, (RB, RB), 1)
            hot.append(
                jnp.concatenate(
                    [(col == lane + p * RB).astype(jnp.float32).astype(jnp.bfloat16) for p in range(n_atoms // RB)], axis=1
                )
            )
        picked = jnp.dot(jnp.concatenate(hot, axis=0), proj[...], preferred_element_type=jnp.float32)
        x = edge_layers(jnp.concatenate(base, axis=0) + picked)
        sent = x.astype(jnp.bfloat16)
        for g, (n, k) in enumerate(zip(ns, ks)):
            xs[rows_of(k), :] = x[g * RB : (g + 1) * RB, :]
            perm = reorder(k)

            def whole_rows():
                moved = jnp.dot(perm, sent[g * RB : (g + 1) * RB, :], preferred_element_type=jnp.float32)
                send[k] = moved.astype(jnp.bfloat16)

                @pl.when(k != me)
                def _():
                    block_copy(k).start()

                @pl.when(k == me)
                def _():
                    own_copy().start()

            def atom_rows(s):
                rows = jnp.dot(hot[g], every_atom(), preferred_element_type=jnp.float32).astype(jnp.bfloat16)
                rows_send[s] = jnp.dot(perm, rows, preferred_element_type=jnp.float32).astype(jnp.bfloat16)
                rows_copy(s).start()

            pl.when(jnp.logical_not(early(n)))(whole_rows)
            for s, e in enumerate(EARLY):
                if e % AHEAD == g:
                    pl.when(n == e)(functools.partial(atom_rows, s))

    for load in loads[6:]:
        load.wait()

    begun = []
    for s, n in enumerate(EARLY):
        k = partner(n, -1)
        arrival(k).wait_recv()
        rows_copy(s).wait_recv()
        near = jnp.dot(rows_recv[s], w_in[...], preferred_element_type=jnp.float32).astype(jnp.bfloat16)
        begun.append(recv[k].astype(jnp.float32) + near.astype(jnp.float32))
    states = edge_layers(jnp.concatenate(begun, axis=0)).astype(jnp.bfloat16)
    for s, n in enumerate(EARLY):
        recv[partner(n, -1)] = states[s * RB : (s + 1) * RB, :]

    @pl.loop(0, n_dst // BEHIND)
    def _(step):
        ns = [step * BEHIND + g for g in range(BEHIND)]
        ks = [partner(n, -1) for n in ns]
        for n, k in zip(ns, ks):

            @pl.when((k != me) & jnp.logical_not(early(n)))
            def _():
                arrival(k).wait_recv()

            @pl.when(k == me)
            def _():
                own_copy().wait()

        came = jnp.concatenate([recv[k] for k in ks], axis=0)
        message = jnp.dot(came, w_rev[...], preferred_element_type=jnp.float32)
        kept, hot = [], []
        for g, k in enumerate(ks):
            slot = lax.broadcasted_iota(jnp.int32, (RB, width), 0)
            total = xs[rows_of(k), :] + message[g * RB : (g + 1) * RB, :]
            result = jnp.where(slot < cnt[k], total, 0.0).astype(jnp.bfloat16)
            edge_out_ref[rows_of(k), :] = result
            kept.append(result)
            sub = lax.broadcasted_iota(jnp.int32, (n_atoms, RB), 0)
            hot.append((sub == targ[k]).astype(jnp.float32).astype(jnp.bfloat16))
        seg[...] += jnp.dot(
            jnp.concatenate(hot, axis=1), jnp.concatenate(kept, axis=0), preferred_element_type=jnp.float32
        )

    down = jnp.dot(seg[...].astype(jnp.bfloat16), w_down[...], preferred_element_type=jnp.float32)
    part[...] = down.astype(jnp.bfloat16).reshape(part.shape)

    def part_copy(d):
        to = far_peer(row, d, 1, n_src)
        return pltpu.make_async_remote_copy(
            src_ref=part.at[to], dst_ref=parts.at[d], send_sem=pt_send.at[d], recv_sem=pt_recv.at[d],
            device_id={"src": to}, device_id_type=MESH,
        )

    @pl.loop(1, n_src)
    def _(d):
        part_copy(d).start()

    agg = part[row].astype(jnp.float32)

    @pl.loop(1, n_src)
    def _(d):
        part_copy(d).wait()

    for d in range(1, n_src):
        agg = agg + parts[d].astype(jnp.float32)
    act = silu(0.3 * agg).astype(jnp.bfloat16)
    update = jnp.dot(act, w_atom[...], preferred_element_type=jnp.float32)
    atom_out_ref[...] = (atoms[row].astype(jnp.float32) + update).astype(jnp.bfloat16)

    @pl.loop(0, n_dst)
    def _(k):
        @pl.when(k != me)
        def _():
            arrival(k).wait_send()

    for s in range(len(EARLY)):
        rows_copy(s).wait_send()


def solution(mesh):
    n_src, n_dst = mesh.shape["src"], mesh.shape["dst"]

    def on_device(edge_in, atom_in, targets, reverse, counts, w_in, gains, w_layers, w_rev, w_down, w_atom):
        slots, width = edge_in.shape
        own, depth = atom_in.shape
        n_atoms = own * n_src
        bf16, f32 = jnp.bfloat16, jnp.float32
        hbm = pl.BlockSpec(memory_space=pltpu.HBM)
        vmem = pl.BlockSpec(memory_space=pltpu.VMEM)
        dma = pltpu.SemaphoreType.DMA
        return pl.pallas_call(
            functools.partial(kernel, n_src, n_dst),
            out_shape=(
                pltpu.VMEM(edge_in.shape, bf16),
                pltpu.VMEM(atom_in.shape, bf16),
            ),
            in_specs=[hbm] * 11,
            out_specs=(vmem, vmem),
            scratch_shapes=[
                pltpu.VMEM((slots, width), bf16),
                pltpu.VMEM((slots, width), f32),
                pltpu.VMEM((n_dst, RB, width), bf16),
                pltpu.VMEM((n_dst, RB, width), bf16),
                pltpu.VMEM((n_src, own, depth), bf16),
                pltpu.VMEM((n_atoms, width), bf16),
                pltpu.VMEM((n_dst, 1, RB), jnp.int32),
                pltpu.VMEM((n_dst, 1, RB), jnp.int32),
                pltpu.SMEM((n_dst,), jnp.int32),
                pltpu.VMEM(gains.shape, f32),
                pltpu.VMEM(w_in.shape, bf16),
                pltpu.VMEM(w_layers.shape, bf16),
                pltpu.VMEM(w_rev.shape, bf16),
                pltpu.VMEM(w_down.shape, bf16),
                pltpu.VMEM(w_atom.shape, bf16),
                pltpu.VMEM((n_atoms, width), f32),
                pltpu.VMEM((n_src, own, depth), bf16),
                pltpu.VMEM((n_src, own, depth), bf16),
                pltpu.VMEM((len(EARLY), RB, depth), bf16),
                pltpu.VMEM((len(EARLY), RB, depth), bf16),
                dma((n_dst,)),
                dma((10,)),
                dma((n_src,)),
                dma((n_src,)),
                dma((n_dst,)),
                dma((n_dst,)),
                dma((n_src,)),
                dma((n_src,)),
                dma((len(EARLY),)),
                dma((len(EARLY),)),
            ],
            compiler_params=pltpu.CompilerParams(
                collective_id=0, has_side_effects=True, vmem_limit_bytes=VMEM_MIB * 2**20
            ),
        )(
            edge_in, atom_in, targets.reshape(n_dst, 1, RB), reverse.reshape(n_dst, 1, RB), counts.reshape(n_dst),
            w_in, gains, w_layers, w_rev, w_down, w_atom,
        )

    both = ("src", "dst")
    in_specs = (
        P(both, None), P(("dst", "src"), None), P(both), P(both), P("src", "dst", None),
        P(), P(), P(), P(), P(), P(),
    )
    out_specs = (P(both, None), P(("dst", "src"), None))
    return jax.shard_map(on_device, mesh=mesh, in_specs=in_specs, out_specs=out_specs, check_vma=False)
```
